32 devices in a mesh: groups: 2 (over x), gx: 16 (over z, y, core).
Axes of the slice: x: 2, y: 2, z: 4, core: 2. Of those that a mesh axis runs over, the one named last changes fastest.
Arguments:
- tokens: bfloat16 [1024, 16384], P('groups', 'gx'), parts along dimension 0, may hold values from -6 to 6
- gate_weight: bfloat16 [16384, 5120], P('gx'), may hold values from -0.046875 to 0.046875
- up_weight: bfloat16 [16384, 5120], P('gx'), may hold values from -0.046875 to 0.046875
- down_weight: bfloat16 [5120, 16384], P(None, 'gx'), may hold values from -0.078125 to 0.078125
Outputs:
- mixed: bfloat16 [1024, 16384], P('groups', 'gx'), parts along dimension 0
The draws below stay inside these ranges and needn't reach their ends.
There are 2 independent parts, one for each index of `groups`. The reference program is written for one: setup_inputs(seed, part) draws one part's arguments, and reference() takes and returns one part's arrays. A program takes and returns all parts, laid end to end along the dimension named above; an argument that names none is the same for every part. Nothing has to cross between parts.
All inputs are finite; a program needn't handle non-finite values.
Results may differ from the reference program's by a relative error of at most 0.0049.
Values may be sent and summed in bfloat16 or wider, within the bound.
No kernel may reach another device: no remote copies, remote signals or barrier semaphores. Data moves between devices by JAX's collectives and lax.ppermute only.
A program may use at most 128 MiB of HBM per device.

```python
import jax
import jax.numpy as jnp

D = 16384
FF = 5120
TOKENS = 512


def spiked(values, rng, source, target, parts, factor):
    owner, partner = [(jnp.arange(values.shape[axis_at]) // (values.shape[axis_at] // parts)).reshape([-1 if axis == axis_at else 1 for axis in range(values.ndim)]) for axis_at in (source, target)]
    chosen = jax.random.permutation(rng, parts)[partner]
    strong = (owner == chosen) | (owner == (partner + parts // 2) % parts)
    return jnp.where(strong, factor * values, values)


def block_levels(key, extent, shards, smallest, high):
    level, own = 1.0, jax.random.fold_in(key, 6)
    for position, blocks in shards:
        draws = jnp.exp(jax.random.uniform(jax.random.fold_in(own, position), (blocks,), jnp.float32, smallest / len(shards), high / len(shards)))
        level = level * jnp.repeat(draws, extent[position] // blocks).reshape([-1 if axis == position else 1 for axis in range(len(extent))])
    return level


def normal_values(rng, extent, scale, limit, cuts=(), kind=jnp.bfloat16):
    array = jax.random.normal(rng, extent, jnp.float32) * scale
    if len(cuts) > 0:
        array = block_levels(rng, extent, cuts, -0.22, 0.18) * array
    return jnp.clip(array, min=-limit, max=limit).astype(kind)


def noise_with(stream_key, shape, deviation, limit, shards, heavy, held_as=jnp.bfloat16):
    array = deviation * jax.random.normal(stream_key, shape, jnp.float32)
    if shards:
        array = array * block_levels(stream_key, shape, shards, -0.22, 0.18)
    return jnp.clip(spiked(array, jax.random.fold_in(stream_key, 3), *heavy), -limit, limit).astype(held_as)


def setup_inputs(seed: int = 0, part: int = 0) -> dict:
    splits = jax.random.split(jax.random.key(seed), 5)
    own_keys = jax.random.split(jax.random.fold_in(splits[4], part), 5)
    return {
        "tokens": noise_with(own_keys[0], (TOKENS, D), 1.0, 6.0, ((1, 16),), (1, 0, 16, 2.0)),
        "gate_weight": normal_values(splits[1], (D, FF), D ** -0.5, 0.046875, ((0, 16),)),
        "up_weight": normal_values(splits[2], (D, FF), D ** -0.5, 0.046875, ((0, 16),)),
        "down_weight": normal_values(splits[3], (FF, D), FF ** -0.5, 0.078125, ((1, 16),)),
    }


def reference(tokens, gate_weight, up_weight, down_weight):
    gate = jnp.dot(tokens, gate_weight, preferred_element_type=jnp.float32)
    up = jnp.dot(tokens, up_weight, preferred_element_type=jnp.float32)
    hidden = (jax.nn.silu(gate) * up).astype(jnp.bfloat16)
    return jnp.dot(hidden, down_weight, preferred_element_type=jnp.float32).astype(jnp.bfloat16)
```

```python
import functools

import jax
import jax.numpy as jnp
from jax import lax
from jax.experimental import pallas as pl
from jax.experimental.pallas import tpu as pltpu
from jax.sharding import PartitionSpec as P

F16, F32, BF16 = jnp.float16, jnp.float32, jnp.bfloat16
PARTS = (10, 10, 10, 10)
CHAIN = True
SCALE = 4.0


def order_of(masks):
    order = [0]
    for m in reversed(masks):
        order = order + [m ^ o for o in order]
    return order


def reorder_kernel(order, back, x_ref, o_ref):
    me = lax.axis_index("gx")
    rows = x_ref.shape[0] // len(order)
    for p, mask in enumerate(order):
        there = pl.ds(pl.multiple_of((me ^ mask) * rows, rows), rows)
        here = slice(p * rows, (p + 1) * rows)
        if back:
            o_ref[there, :] = x_ref[here, :]
        else:
            o_ref[here, :] = x_ref[there, :] * jnp.asarray(SCALE, x_ref.dtype)


def reorder(x, order, back):
    return pl.pallas_call(
        functools.partial(reorder_kernel, order, back),
        out_shape=jax.ShapeDtypeStruct(x.shape, x.dtype),
        in_specs=[pl.BlockSpec(memory_space=pltpu.VMEM)],
        out_specs=pl.BlockSpec(memory_space=pltpu.VMEM),
    )(x)


def schedule(chunks, levels):
    sends = [11, 59, 30, 22] if levels == 4 else [11] + [40] * (levels - 1)
    shares = [p / sum(PARTS) for p in PARTS]
    keys = []
    start = 0.0
    for c, share in enumerate(shares):
        t = start
        keys.append((t, c, 0))
        for s in range(levels):
            t += 4 + sends[s] * share
            keys.append((t, c, s + 1))
        for s in reversed(range(levels)):
            t += 4 + sends[s] * share / 2
            keys.append((t, c, 2 * levels - s))
        start += 59 * share
    return [(c, s) for _, c, s in sorted(keys)]


def on_device(n, tokens, gate_weight, up_weight, down_weight):
    masks = [1 << k for k in range(n.bit_length() - 1)]
    levels = len(masks)
    order = order_of(masks)
    width = gate_weight.shape[1]
    x = reorder(tokens, order, False)
    total = [None, None]
    last = None
    state = {}
    bounds = [sum(PARTS[:c]) * width // sum(PARTS) for c in range(len(PARTS) + 1)]

    def swap(v, mask):
        return lax.ppermute(v, "gx", [(i, i ^ mask) for i in range(n)])

    for c, stage in schedule(len(PARTS), levels):
        cols = slice(bounds[c], bounds[c + 1])
        w = bounds[c + 1] - bounds[c]
        ins = state.pop(c, x)
        if CHAIN and last is not None:
            ins, _ = lax.optimization_barrier((ins, last))
        if stage == 0:
            gate = jnp.dot(ins, gate_weight[:, cols], preferred_element_type=F32)
            up = jnp.dot(ins, up_weight[:, cols], preferred_element_type=F32)
            acc = jnp.concatenate([gate, up], axis=1)
        elif stage <= levels:
            acc, got = ins
            acc = acc + got.astype(F32)
        else:
            hidden, got = ins
        if stage < levels:
            half = acc.shape[0] // 2
            send = acc[half:].astype(F16)
            state[c] = (acc[:half], swap(send, masks[stage]))
            last = send
        elif stage == levels:
            acc = acc * (1 / SCALE)
            hidden = (jax.nn.silu(acc[:, :w]) * acc[:, w:]).astype(BF16)
            state[c] = (hidden, swap(hidden, masks[-1]))
            last = hidden
        elif stage < 2 * levels:
            hidden = jnp.concatenate([hidden, got], axis=0)
            last = hidden
            state[c] = (hidden, swap(hidden, masks[2 * levels - 1 - stage]))
            if stage == 2 * levels - 1:
                lo = jnp.dot(hidden, down_weight[cols], preferred_element_type=F32)
                total[0] = lo if total[0] is None else total[0] + lo
        else:
            hi = jnp.dot(got, down_weight[cols], preferred_element_type=F32)
            total[1] = hi if total[1] is None else total[1] + hi
            last = total[1][:8, :128]
    result = jnp.concatenate([t.astype(BF16) for t in total], axis=0)
    return reorder(result, order, True)


def solution(mesh):
    placed = (P("groups", "gx"), P("gx", None), P("gx", None), P(None, "gx"))
    return jax.shard_map(
        functools.partial(on_device, mesh.shape["gx"]),
        mesh=mesh, in_specs=placed, out_specs=P("groups", "gx"), check_vma=False,
    )
```

```python
import functools

import jax
import jax.numpy as jnp
from jax import lax
from jax.experimental import pallas as pl
from jax.experimental.pallas import tpu as pltpu
from jax.sharding import PartitionSpec as P

F16, F32, BF16 = jnp.float16, jnp.float32, jnp.bfloat16
PARTS = (4,4,4,4,4)
SCALE = 4.0
FREE = pl.CostEstimate(flops=0, bytes_accessed=0, transcendentals=0)


def order_of(masks):
    order = [0]
    for m in reversed(masks):
        order = order + [m ^ o for o in order]
    return order


def schedule(levels, chunks):
    steps = [(0, 0), (1, 0), (0, 1), *((c, 0) for c in range(2, chunks)), (1, 1)]
    for tick in range(chunks + 2 * levels):
        steps += [(tick, 2), (tick + 2, 1), *((tick + 2 - s, s) for s in range(3, 2 * levels + 1))]
    return [(c, s) for c, s in steps if 0 <= c < chunks]


def reorder_kernel(order, x_ref, o_ref):
    me = lax.axis_index("gx")
    rows = x_ref.shape[0] // len(order)
    for p, mask in enumerate(order):
        there = pl.ds(pl.multiple_of((me ^ mask) * rows, rows), rows)
        o_ref[p * rows : (p + 1) * rows, :] = x_ref[there, :] * jnp.asarray(SCALE, BF16)


def reorder(x, order):
    return pl.pallas_call(
        functools.partial(reorder_kernel, order),
        out_shape=jax.ShapeDtypeStruct(x.shape, x.dtype),
        in_specs=[pl.BlockSpec(memory_space=pltpu.VMEM)],
        out_specs=pl.BlockSpec(memory_space=pltpu.VMEM),
        cost_estimate=FREE,
    )(x)


def last_kernel(order, lo_ref, hi_ref, hidden_ref, down_ref, out_ref):
    me = lax.axis_index("gx")
    rows = out_ref.shape[0] // len(order)
    half = len(order) // 2
    hi = hi_ref[...] + jnp.dot(hidden_ref[...], down_ref[...], preferred_element_type=F32)
    for p, mask in enumerate(order):
        there = pl.ds(pl.multiple_of((me ^ mask) * rows, rows), rows)
        if p < half:
            block = lo_ref[p * rows : (p + 1) * rows, :]
        else:
            block = hi[(p - half) * rows : (p - half + 1) * rows]
        out_ref[there, :] = block.astype(BF16)


def finish(order, lo, hi, hidden, down_weight):
    rows, w = hidden.shape
    columns = down_weight.shape[1]
    tile = min(512, columns)
    return pl.pallas_call(
        functools.partial(last_kernel, order),
        grid=(columns // tile,),
        in_specs=[
            pl.BlockSpec((rows, tile), lambda j: (0, j)),
            pl.BlockSpec((rows, tile), lambda j: (0, j)),
            pl.BlockSpec((rows, w), lambda j: (0, 0)),
            pl.BlockSpec((w, tile), lambda j: (0, j)),
        ],
        out_specs=pl.BlockSpec((2 * rows, tile), lambda j: (0, j)),
        out_shape=jax.ShapeDtypeStruct((2 * rows, columns), BF16),
        cost_estimate=FREE,
        compiler_params=pltpu.CompilerParams(vmem_limit_bytes=24 << 20),
    )(lo, hi, hidden, down_weight)


def on_device(n, tokens, gate_weight, up_weight, down_weight):
    masks = [1 << k for k in range(n.bit_length() - 1)]
    levels = len(masks)
    order = order_of(masks)
    width = gate_weight.shape[1]
    widths = [p * width // sum(PARTS) for p in PARTS]
    starts = [sum(widths[c + 1 :]) for c in range(len(PARTS))]
    total, state, last, result = [None, None], {}, None, None
    steps = schedule(levels, len(PARTS))
    final = len(PARTS) - 1
    steps = [p for p in steps if p != (final, 2 * levels)] + [(final, 2 * levels)]

    def swap(v, mask):
        return lax.ppermute(v, "gx", [(i, i ^ mask) for i in range(n)])

    def split(v):
        half = v.shape[1] // 2
        return v[:, :half], v[:, half:]

    def add(v, got):
        return v.astype(F32) + got.astype(F32)

    x = reorder(tokens, order)
    x = [jnp.dot(x, v, preferred_element_type=F32).astype(F16) for v in (gate_weight, up_weight)]
    for c, stage in steps:
        at, w = starts[c], widths[c]
        cols = slice(at, at + w)
        ins = state.pop(c, x)
        if last is not None:
            ins, _ = lax.optimization_barrier((ins, last))
        if stage == 0:
            acc = jnp.stack([ins[0][:, cols], ins[1][:, cols]])
            keep, send = split(acc)
        elif stage < levels:
            (keep, send), (got_keep, got_send) = split(ins[0]), split(ins[1])
            keep, send = add(keep, got_keep), add(send, got_send)
        if stage < levels:
            send = send.astype(F16)
            state[c] = (keep, swap(send, masks[stage]))
            last = send
        elif stage == levels:
            acc = add(*ins) * (1 / SCALE)
            last = (jax.nn.silu(acc[0]) * acc[1]).astype(BF16)
            state[c] = (last, swap(last, masks[-1]))
        elif stage < 2 * levels:
            last = jnp.concatenate(ins, axis=0)
            state[c] = (last, swap(last, masks[2 * levels - 1 - stage]))
            if stage == 2 * levels - 1:
                lo = jnp.dot(last, down_weight[cols], preferred_element_type=F32)
                total[0] = lo if total[0] is None else total[0] + lo
        elif c == final:
            result = finish(order, total[0], total[1], ins[1], down_weight)
        else:
            hi = jnp.dot(ins[1], down_weight[cols], preferred_element_type=F32)
            total[1] = hi if total[1] is None else total[1] + hi
            last = ins[1]
    return result


def solution(mesh):
    placed = (P("groups", "gx"), P("gx", None), P("gx", None), P(None, "gx"))
    return jax.shard_map(
        functools.partial(on_device, mesh.shape["gx"]),
        mesh=mesh, in_specs=placed, out_specs=P("groups", "gx"), check_vma=False,
    )
```

```python
import functools

import jax
import jax.numpy as jnp
from jax import lax
from jax.experimental import pallas as pl
from jax.experimental.pallas import tpu as pltpu
from jax.sharding import PartitionSpec as P

F16, F32, BF16 = jnp.float16, jnp.float32, jnp.bfloat16
PARTS = (4,4,4,4,4)
SUM_Z_FIRST = (1,)
GATHER_Z_LAST = ()
EARLY = ((2, 1),)
SCALE = 4.0
FREE = pl.CostEstimate(flops=0, bytes_accessed=0, transcendentals=0)


def order_of(masks):
    order = [0]
    for m in reversed(masks):
        order = order + [m ^ o for o in order]
    return order


def schedule(levels, chunks):
    steps = [(0, 0), (1, 0), (0, 1), *((c, 0) for c in range(2, chunks)), (1, 1), *EARLY]
    for tick in range(chunks + 2 * levels):
        steps += [(tick, 2), *(() if (tick + 2, 1) in EARLY else ((tick + 2, 1),)), *((tick + 2 - s, s) for s in range(3, 2 * levels + 1))]
    return [(c, s) for c, s in steps if 0 <= c < chunks]


def reorder_kernel(order, x_ref, o_ref):
    me = lax.axis_index("gx")
    rows = x_ref.shape[0] // len(order)
    for p, mask in enumerate(order):
        there = pl.ds(pl.multiple_of((me ^ mask) * rows, rows), rows)
        o_ref[p * rows : (p + 1) * rows, :] = x_ref[there, :] * jnp.asarray(SCALE, BF16)


def reorder(x, order):
    return pl.pallas_call(
        functools.partial(reorder_kernel, order),
        out_shape=jax.ShapeDtypeStruct(x.shape, x.dtype),
        in_specs=[pl.BlockSpec(memory_space=pltpu.VMEM)],
        out_specs=pl.BlockSpec(memory_space=pltpu.VMEM),
        cost_estimate=FREE,
    )(x)


def last_kernel(order, lo_ref, hi_ref, hidden_ref, down_ref, out_ref):
    me = lax.axis_index("gx")
    rows = out_ref.shape[0] // len(order)
    half = len(order) // 2
    hi = hi_ref[...] + jnp.dot(hidden_ref[...], down_ref[...], preferred_element_type=F32)
    for p, mask in enumerate(order):
        there = pl.ds(pl.multiple_of((me ^ mask) * rows, rows), rows)
        if p < half:
            block = lo_ref[p * rows : (p + 1) * rows, :]
        else:
            block = hi[(p - half) * rows : (p - half + 1) * rows]
        out_ref[there, :] = block.astype(BF16)


def finish(order, lo, hi, hidden, down_weight):
    rows, w = hidden.shape
    columns = down_weight.shape[1]
    tile = min(512, columns)
    return pl.pallas_call(
        functools.partial(last_kernel, order),
        grid=(columns // tile,),
        in_specs=[
            pl.BlockSpec((rows, tile), lambda j: (0, j)),
            pl.BlockSpec((rows, tile), lambda j: (0, j)),
            pl.BlockSpec((rows, w), lambda j: (0, 0)),
            pl.BlockSpec((w, tile), lambda j: (0, j)),
        ],
        out_specs=pl.BlockSpec((2 * rows, tile), lambda j: (0, j)),
        out_shape=jax.ShapeDtypeStruct((2 * rows, columns), BF16),
        cost_estimate=FREE,
        compiler_params=pltpu.CompilerParams(vmem_limit_bytes=24 << 20),
    )(lo, hi, hidden, down_weight)


def on_device(n, tokens, gate_weight, up_weight, down_weight):
    masks = [1 << k for k in range(n.bit_length() - 1)]
    levels = len(masks)
    order = order_of(masks)
    width = gate_weight.shape[1]
    widths = [p * width // sum(PARTS) for p in PARTS]
    starts = [sum(widths[c + 1 :]) for c in range(len(PARTS))]
    total, state, last, result = [None, None], {}, None, None
    steps = schedule(levels, len(PARTS))
    final = len(PARTS) - 1
    steps = [p for p in steps if p != (final, 2 * levels)] + [(final, 2 * levels)]

    def swap(v, mask):
        return lax.ppermute(v, "gx", [(i, i ^ mask) for i in range(n)])

    def split(v, level):
        first, rows, w = v.shape
        v = v.reshape(first, 2**level, 2, rows >> (level + 1), w)
        return (v[:, :, k].reshape(first, rows // 2, w) for k in (0, 1))

    def turned(chunks):
        turn = [0, 2, 1, *range(3, levels)] if levels > 2 else list(range(levels))
        return [turn if c in chunks else list(range(levels)) for c in range(len(PARTS))]

    sums, gathers = turned(SUM_Z_FIRST), turned(GATHER_Z_LAST)

    def join(parts, inner):
        if inner:
            parts = [half for pair in zip(*(jnp.split(v, 2) for v in parts)) for half in pair]
        return jnp.concatenate(parts, axis=0)

    def add(v, got):
        return v.astype(F32) + got.astype(F32)

    x = reorder(tokens, order)
    x = [jnp.dot(x, v, preferred_element_type=F32).astype(F16) for v in (gate_weight, up_weight)]
    for c, stage in steps:
        at, w = starts[c], widths[c]
        cols = slice(at, at + w)
        ins = state.pop(c, x)
        if last is not None:
            ins, _ = lax.optimization_barrier((ins, last))
        if stage == 0:
            acc = jnp.stack([ins[0][:, cols], ins[1][:, cols]])
            keep, send = split(acc, 0)
        elif stage < levels:
            skip = 1 if sums[c][stage] > stage else 0
            (keep, send), (got_keep, got_send) = split(ins[0], skip), split(ins[1], skip)
            keep, send = add(keep, got_keep), add(send, got_send)
        if stage < levels:
            send = send.astype(F16)
            state[c] = (keep, swap(send, masks[sums[c][stage]]))
            last = send
        elif stage == levels:
            acc = add(*ins) * (1 / SCALE)
            last = (jax.nn.silu(acc[0]) * acc[1]).astype(BF16)
            state[c] = (last, swap(last, masks[-1]))
        elif stage < 2 * levels:
            level = 2 * levels - stage
            last = join(ins, gathers[c][level] > level)
            state[c] = (last, swap(last, masks[gathers[c][level - 1]]))
            if stage == 2 * levels - 1:
                lo = jnp.dot(last, down_weight[cols], preferred_element_type=F32)
                total[0] = lo if total[0] is None else total[0] + lo
                last = (last, total[0])
        elif c == final:
            result = finish(order, total[0], total[1], ins[1], down_weight)
        else:
            hi = jnp.dot(ins[1], down_weight[cols], preferred_element_type=F32)
            total[1] = hi if total[1] is None else total[1] + hi
            last = total[1]
    return result


def solution(mesh):
    placed = (P("groups", "gx"), P("gx", None), P("gx", None), P(None, "gx"))
    return jax.shard_map(
        functools.partial(on_device, mesh.shape["gx"]),
        mesh=mesh, in_specs=placed, out_specs=P("groups", "gx"), check_vma=False,
    )
```

```python
import functools

import jax
import jax.numpy as jnp
from jax import lax
from jax.experimental import pallas as pl
from jax.experimental.pallas import tpu as pltpu
from jax.sharding import PartitionSpec as P

F16, F32, BF16 = jnp.float16, jnp.float32, jnp.bfloat16
PARTS = (4,4,4,4,4)
SUM_Z_FIRST = (2,)
GATHER_Z_LAST = ()
EARLY = ((2, 1),)
SCALE = 4.0
FREE = pl.CostEstimate(flops=0, bytes_accessed=0, transcendentals=0)


def order_of(masks):
    order = [0]
    for m in reversed(masks):
        order = order + [m ^ o for o in order]
    return order


def schedule(levels, chunks):
    steps = [(0, 0), (1, 0), (0, 1), *((c, 0) for c in range(2, chunks)), (1, 1), *EARLY]
    for tick in range(chunks + 2 * levels):
        steps += [(tick, 2), *(() if (tick + 2, 1) in EARLY else ((tick + 2, 1),)), *((tick + 2 - s, s) for s in range(3, 2 * levels + 1))]
    return [(c, s) for c, s in steps if 0 <= c < chunks]


def reorder_kernel(order, x_ref, o_ref):
    me = lax.axis_index("gx")
    rows = x_ref.shape[0] // len(order)
    for p, mask in enumerate(order):
        there = pl.ds(pl.multiple_of((me ^ mask) * rows, rows), rows)
        o_ref[p * rows : (p + 1) * rows, :] = x_ref[there, :] * jnp.asarray(SCALE, BF16)


def reorder(x, order):
    return pl.pallas_call(
        functools.partial(reorder_kernel, order),
        out_shape=jax.ShapeDtypeStruct(x.shape, x.dtype),
        in_specs=[pl.BlockSpec(memory_space=pltpu.VMEM)],
        out_specs=pl.BlockSpec(memory_space=pltpu.VMEM),
        cost_estimate=FREE,
    )(x)


def last_kernel(order, lo_ref, hi_ref, hidden_ref, down_ref, out_ref):
    me = lax.axis_index("gx")
    rows = out_ref.shape[0] // len(order)
    half = len(order) // 2
    hi = hi_ref[...] + jnp.dot(hidden_ref[...], down_ref[...], preferred_element_type=F32)
    for p, mask in enumerate(order):
        there = pl.ds(pl.multiple_of((me ^ mask) * rows, rows), rows)
        if p < half:
            block = lo_ref[p * rows : (p + 1) * rows, :]
        else:
            block = hi[(p - half) * rows : (p - half + 1) * rows]
        out_ref[there, :] = block.astype(BF16)


def finish(order, lo, hi, hidden, down_weight):
    rows, w = hidden.shape
    columns = down_weight.shape[1]
    tile = min(512, columns)
    return pl.pallas_call(
        functools.partial(last_kernel, order),
        grid=(columns // tile,),
        in_specs=[
            pl.BlockSpec((rows, tile), lambda j: (0, j)),
            pl.BlockSpec((rows, tile), lambda j: (0, j)),
            pl.BlockSpec((rows, w), lambda j: (0, 0)),
            pl.BlockSpec((w, tile), lambda j: (0, j)),
        ],
        out_specs=pl.BlockSpec((2 * rows, tile), lambda j: (0, j)),
        out_shape=jax.ShapeDtypeStruct((2 * rows, columns), BF16),
        cost_estimate=FREE,
        compiler_params=pltpu.CompilerParams(vmem_limit_bytes=24 << 20),
    )(lo, hi, hidden, down_weight)


def on_device(n, tokens, gate_weight, up_weight, down_weight):
    masks = [1 << k for k in range(n.bit_length() - 1)]
    levels = len(masks)
    order = order_of(masks)
    width = gate_weight.shape[1]
    widths = [p * width // sum(PARTS) for p in PARTS]
    starts = [sum(widths[c + 1 :]) for c in range(len(PARTS))]
    total, state, last, result = [None, None], {}, None, None
    steps = schedule(levels, len(PARTS))
    final = len(PARTS) - 1
    steps = [p for p in steps if p != (final, 2 * levels)] + [(final, 2 * levels)]

    def swap(v, mask):
        return lax.ppermute(v, "gx", [(i, i ^ mask) for i in range(n)])

    def split(v, level):
        first, rows, w = v.shape
        v = v.reshape(first, 2**level, 2, rows >> (level + 1), w)
        return (v[:, :, k].reshape(first, rows // 2, w) for k in (0, 1))

    def turned(chunks):
        turn = [0, 2, 1, *range(3, levels)] if levels > 2 else list(range(levels))
        return [turn if c in chunks else list(range(levels)) for c in range(len(PARTS))]

    sums, gathers = turned(SUM_Z_FIRST), turned(GATHER_Z_LAST)

    def join(parts, inner):
        if inner:
            parts = [half for pair in zip(*(jnp.split(v, 2) for v in parts)) for half in pair]
        return jnp.concatenate(parts, axis=0)

    def add(v, got):
        return v.astype(F32) + got.astype(F32)

    x = reorder(tokens, order)
    x = [jnp.dot(x, v, preferred_element_type=F32).astype(F16) for v in (gate_weight, up_weight)]
    for c, stage in steps:
        at, w = starts[c], widths[c]
        cols = slice(at, at + w)
        ins = state.pop(c, x)
        if last is not None:
            ins, _ = lax.optimization_barrier((ins, last))
        if stage == 0:
            acc = jnp.stack([ins[0][:, cols], ins[1][:, cols]])
            keep, send = split(acc, 0)
        elif stage < levels:
            skip = 1 if sums[c][stage] > stage else 0
            (keep, send), (got_keep, got_send) = split(ins[0], skip), split(ins[1], skip)
            keep, send = add(keep, got_keep), add(send, got_send)
        if stage < levels:
            send = send.astype(F16)
            state[c] = (keep, swap(send, masks[sums[c][stage]]))
            last = send
        elif stage == levels:
            acc = add(*ins) * (1 / SCALE)
            last = (jax.nn.silu(acc[0]) * acc[1]).astype(BF16)
            state[c] = (last, swap(last, masks[-1]))
        elif stage < 2 * levels:
            level = 2 * levels - stage
            last = join(ins, gathers[c][level] > level)
            state[c] = (last, swap(last, masks[gathers[c][level - 1]]))
            if stage == 2 * levels - 1:
                lo = jnp.dot(last, down_weight[cols], preferred_element_type=F32)
                total[0] = lo if total[0] is None else total[0] + lo
                last = (last, total[0])
        elif c == final:
            result = finish(order, total[0], total[1], ins[1], down_weight)
        else:
            hi = jnp.dot(ins[1], down_weight[cols], preferred_element_type=F32)
            total[1] = hi if total[1] is None else total[1] + hi
            last = total[1]
    return result


def solution(mesh):
    placed = (P("groups", "gx"), P("gx", None), P("gx", None), P(None, "gx"))
    return jax.shard_map(
        functools.partial(on_device, mesh.shape["gx"]),
        mesh=mesh, in_specs=placed, out_specs=P("groups", "gx"), check_vma=False,
    )
```

```python
import functools

import jax
import jax.numpy as jnp
from jax import lax
from jax.experimental import pallas as pl
from jax.experimental.pallas import tpu as pltpu
from jax.sharding import PartitionSpec as P

F16, F32, BF16 = jnp.float16, jnp.float32, jnp.bfloat16
PARTS = (4,4,4,4,4)
SUM_Z_FIRST = (1,)
GATHER_Z_LAST = ()
EARLY = ((2, 1),)
SCALE = 4.0
FREE = pl.CostEstimate(flops=0, bytes_accessed=0, transcendentals=0)


def order_of(masks):
    order = [0]
    for m in reversed(masks):
        order = order + [m ^ o for o in order]
    return order


def schedule(levels, chunks):
    steps = [(0, 0), (1, 0), (0, 1), (2, 0), (1, 1), (3, 0), *EARLY, *((c, 0) for c in range(4, chunks))]
    for tick in range(chunks + 2 * levels):
        steps += [(tick, 2), *(() if (tick + 2, 1) in EARLY else ((tick + 2, 1),)), *((tick + 2 - s, s) for s in range(3, 2 * levels + 1))]
    return [(c, s) for c, s in steps if 0 <= c < chunks]


def reorder_kernel(order, x_ref, o_ref):
    me = lax.axis_index("gx")
    rows = x_ref.shape[0] // len(order)
    for p, mask in enumerate(order):
        there = pl.ds(pl.multiple_of((me ^ mask) * rows, rows), rows)
        o_ref[p * rows : (p + 1) * rows, :] = x_ref[there, :] * jnp.asarray(SCALE, BF16)


def reorder(x, order):
    return pl.pallas_call(
        functools.partial(reorder_kernel, order),
        out_shape=jax.ShapeDtypeStruct(x.shape, x.dtype),
        in_specs=[pl.BlockSpec(memory_space=pltpu.VMEM)],
        out_specs=pl.BlockSpec(memory_space=pltpu.VMEM),
        cost_estimate=FREE,
    )(x)


def last_kernel(order, lo_ref, hi_ref, hidden_ref, down_ref, out_ref):
    me = lax.axis_index("gx")
    rows = out_ref.shape[0] // len(order)
    half = len(order) // 2
    hi = hi_ref[...] + jnp.dot(hidden_ref[...], down_ref[...], preferred_element_type=F32)
    for p, mask in enumerate(order):
        there = pl.ds(pl.multiple_of((me ^ mask) * rows, rows), rows)
        if p < half:
            block = lo_ref[p * rows : (p + 1) * rows, :]
        else:
            block = hi[(p - half) * rows : (p - half + 1) * rows]
        out_ref[there, :] = block.astype(BF16)


def finish(order, lo, hi, hidden, down_weight):
    rows, w = hidden.shape
    columns = down_weight.shape[1]
    tile = min(512, columns)
    return pl.pallas_call(
        functools.partial(last_kernel, order),
        grid=(columns // tile,),
        in_specs=[
            pl.BlockSpec((rows, tile), lambda j: (0, j)),
            pl.BlockSpec((rows, tile), lambda j: (0, j)),
            pl.BlockSpec((rows, w), lambda j: (0, 0)),
            pl.BlockSpec((w, tile), lambda j: (0, j)),
        ],
        out_specs=pl.BlockSpec((2 * rows, tile), lambda j: (0, j)),
        out_shape=jax.ShapeDtypeStruct((2 * rows, columns), BF16),
        cost_estimate=FREE,
        compiler_params=pltpu.CompilerParams(vmem_limit_bytes=24 << 20),
    )(lo, hi, hidden, down_weight)


def on_device(n, tokens, gate_weight, up_weight, down_weight):
    masks = [1 << k for k in range(n.bit_length() - 1)]
    levels = len(masks)
    order = order_of(masks)
    width = gate_weight.shape[1]
    widths = [p * width // sum(PARTS) for p in PARTS]
    starts = [sum(widths[c + 1 :]) for c in range(len(PARTS))]
    total, state, last, result = [None, None], {}, None, None
    steps = schedule(levels, len(PARTS))
    final = len(PARTS) - 1
    steps = [p for p in steps if p != (final, 2 * levels)] + [(final, 2 * levels)]

    def swap(v, mask):
        return lax.ppermute(v, "gx", [(i, i ^ mask) for i in range(n)])

    def split(v, level):
        first, rows, w = v.shape
        v = v.reshape(first, 2**level, 2, rows >> (level + 1), w)
        return (v[:, :, k].reshape(first, rows // 2, w) for k in (0, 1))

    def turned(chunks):
        turn = [0, 2, 1, *range(3, levels)] if levels > 2 else list(range(levels))
        return [turn if c in chunks else list(range(levels)) for c in range(len(PARTS))]

    sums, gathers = turned(SUM_Z_FIRST), turned(GATHER_Z_LAST)

    def join(parts, inner):
        if inner:
            parts = [half for pair in zip(*(jnp.split(v, 2) for v in parts)) for half in pair]
        return jnp.concatenate(parts, axis=0)

    def add(v, got):
        return v.astype(F32) + got.astype(F32)

    x = reorder(tokens, order)
    x = [jnp.dot(x, v, preferred_element_type=F32).astype(F16) for v in (gate_weight, up_weight)]
    for c, stage in steps:
        at, w = starts[c], widths[c]
        cols = slice(at, at + w)
        ins = state.pop(c, x)
        if last is not None:
            ins, _ = lax.optimization_barrier((ins, last))
        if stage == 0:
            acc = jnp.stack([ins[0][:, cols], ins[1][:, cols]])
            keep, send = split(acc, 0)
        elif stage < levels:
            skip = 1 if sums[c][stage] > stage else 0
            (keep, send), (got_keep, got_send) = split(ins[0], skip), split(ins[1], skip)
            keep, send = add(keep, got_keep), add(send, got_send)
        if stage < levels:
            send = send.astype(F16)
            state[c] = (keep, swap(send, masks[sums[c][stage]]))
            last = send
        elif stage == levels:
            acc = add(*ins) * (1 / SCALE)
            last = (jax.nn.silu(acc[0]) * acc[1]).astype(BF16)
            state[c] = (last, swap(last, masks[-1]))
        elif stage < 2 * levels:
            level = 2 * levels - stage
            last = join(ins, gathers[c][level] > level)
            state[c] = (last, swap(last, masks[gathers[c][level - 1]]))
            if stage == 2 * levels - 1:
                lo = jnp.dot(last, down_weight[cols], preferred_element_type=F32)
                total[0] = lo if total[0] is None else total[0] + lo
                last = (last, total[0])
        elif c == final:
            result = finish(order, total[0], total[1], ins[1], down_weight)
        else:
            hi = jnp.dot(ins[1], down_weight[cols], preferred_element_type=F32)
            total[1] = hi if total[1] is None else total[1] + hi
            last = total[1]
    return result


def solution(mesh):
    placed = (P("groups", "gx"), P("gx", None), P("gx", None), P(None, "gx"))
    return jax.shard_map(
        functools.partial(on_device, mesh.shape["gx"]),
        mesh=mesh, in_specs=placed, out_specs=P("groups", "gx"), check_vma=False,
    )
```
